1024 devices in a mesh: node: 128 (over z, x, core), local: 8 (over y).
Axes of the slice: x: 8, y: 8, z: 8, core: 2. Of those that a mesh axis runs over, the one named last changes fastest.
Arguments:
- tokens: bfloat16 [2048, 4096], P('node', 'local'), may hold values from -6 to 6
- grad_out: bfloat16 [2048, 4096], P('node', 'local'), may hold values from -6 to 6
- gates: float32 [2048, 8], P('node'), may hold values from 0.1 to 1
- expert_ids: int32 [2048, 8], P('node'), may hold values from 0 to 127, all different within a row; in each aligned block of 16 rows (0 to 15, 16 to 31, ...) at most 2 rows name the same one
- w_gate: bfloat16 [128, 4096, 1024], P('node', 'local'), may hold values from -0.09375 to 0.09375
- w_up: bfloat16 [128, 4096, 1024], P('node', 'local'), may hold values from -0.09375 to 0.09375
- w_down: bfloat16 [128, 1024, 4096], P('node', None, 'local'), may hold values from -0.046875 to 0.046875
Outputs:
- grad_tokens: bfloat16 [2048, 4096], P('node', 'local')
- grad_gates: bfloat16 [2048, 8], P('node')
The draws below stay inside these ranges and needn't reach their ends.
Inputs may be any that keep to these rules, and one draw needn't show every extreme that they name: `expert_ids`: each row names 8 different experts. Among the 16 rows of one node rank no expert is named by more than 2 rows, a bound that some block reaches.
All inputs are finite; a program needn't handle non-finite values.
Results may differ from the reference program's by a relative error of at most 0.0057.
Values may be sent and summed in bfloat16 or wider, within the bound.
No kernel may reach another device: no remote copies, remote signals or barrier semaphores. Data moves between devices by JAX's collectives and lax.ppermute only.
A program may use at most 32 MiB of HBM per device.

```python
import math
import jax
import jax.numpy as jnp
import numpy as np
from jax import lax

D = 4096
FF = 1024
TOPK = 8
TOK_NODE = 16
EXPERTS = 128
CAP = 2
TOKENS = 2048
N_NODE = 128


def block_scale(own_key, dims, split, smallest, top_value):
    factor_of, own = 1.0, jax.random.fold_in(own_key, 6)
    for dim, shards_of in split:
        draws = jnp.exp(jax.random.uniform(jax.random.fold_in(own, dim), (shards_of,), jnp.float32, smallest / len(split), top_value / len(split)))
        factor_of = factor_of * jnp.repeat(draws, dims[dim] // shards_of).reshape([-1 if axis == dim else 1 for axis in range(len(dims))])
    return factor_of


def deal_out(rng, own, number, rows, count, top, bound, skew):
    order = jax.random.permutation(rng, count)
    packed, common = portions_of(count, rows * top, bound, skew, True), portions_of(count, rows * top, bound, skew, False)
    places = jnp.arange(count)

    def named(tallies, offset_by):
        used = int((tallies > 0).sum())
        fixed = max(1, used // 4)
        moved = fixed + (places - fixed + offset_by * (used - fixed)) % max(1, count - fixed)
        return jnp.zeros((count,), jnp.int32).at[order[jnp.where(places < fixed, places, moved)]].set(jnp.asarray(tallies, jnp.int32))

    tallies = jnp.where(number % 4 == 0, named(packed, number // 4), named(common, number - number // 4 - 1))
    mixed = jax.random.permutation(jax.random.fold_in(own, 3), count)
    source_of, taker = mixed[0:count // 2 * 2:2], mixed[1:count // 2 * 2:2]
    slack = jnp.minimum(tallies[source_of] - 1, bound - tallies[taker]) // 2
    slack = jnp.where((source_of == order[0]) | (taker == order[0]) | (tallies[taker] == 0), 0, jnp.maximum(slack, 0))
    moved = jax.random.randint(jax.random.fold_in(own, 4), (count // 2,), 0, 1 << 20) % (slack + 1)
    tallies = tallies.at[source_of].add(-moved).at[taker].add(moved)
    labels = jnp.searchsorted(jnp.cumsum(tallies), jnp.arange(rows * top), side="right").astype(jnp.int32)
    grid = labels.reshape(top, rows).T
    grid = grid[jax.random.permutation(jax.random.fold_in(own, 1), rows)]
    offset_by = jax.random.randint(jax.random.fold_in(own, 2), (rows, 1), 0, top)
    return jnp.take_along_axis(grid, (jnp.arange(top)[None, :] + offset_by) % top, axis=1)


def portions_of(count, total, limit, slope, full):
    portions = [(1 << 20) // math.isqrt(rank ** slope) + 1 for rank in range(1, count + 1)]
    largest = limit if full else min(limit, max(-(-total // count), total * portions[0] // sum(portions)))
    least = 1 if total - largest >= count - 1 else 0
    holding, spare = [largest] + [least] * (count - 1), total - largest - least * (count - 1)
    while spare > 0:
        free = [i for i in range(1, count) if holding[i] < largest] or [i for i in range(1, count) if holding[i] < limit]
        mass, remaining = sum([portions[i] for i in free]), spare
        for i in free:
            extra = min(limit - holding[i], max(1, remaining * portions[i] // mass), spare)
            holding[i] = holding[i] + extra
            spare = spare - extra
    return np.array(holding)


def centred(rng, dims, width, bound, shards=(), held_as=jnp.bfloat16):
    entries = width * jax.random.normal(rng, dims, jnp.float32)
    if shards:
        entries = entries * block_scale(rng, dims, shards, -0.22, 0.18)
    return jnp.clip(entries, -bound, bound).astype(held_as)


def setup_inputs(seed: int = 0) -> dict:
    key_of = jax.random.split(jax.random.key(seed), 8)
    tokens = centred(key_of[0], (TOKENS, D), 1.0, 6.0, ((0, 128), (1, 8)))
    grad_out = centred(key_of[1], (TOKENS, D), 1.0, 6.0, ((0, 128), (1, 8)))
    gates = jnp.clip(jnp.exp(math.log(1.0) - 2.3025851 * jax.random.uniform(key_of[2], (TOKENS, TOPK), jnp.float32) ** block_scale(key_of[2], (TOKENS, TOPK), ((0, 128),), -0.2, 0.2)), 0.1, 1.0)
    expert_ids_keys = jax.random.split(jax.random.fold_in(key_of[3], 1), TOKENS // TOK_NODE)
    expert_ids_turns = jax.random.permutation(jax.random.fold_in(key_of[3], 3), TOKENS // TOK_NODE)
    expert_ids = jax.vmap(lambda own, number: deal_out(jax.random.fold_in(key_of[3], 2), own, number, TOK_NODE, EXPERTS, TOPK, CAP, 2))(expert_ids_keys, expert_ids_turns).reshape((TOKENS, TOPK))
    w_gate = centred(key_of[4], (EXPERTS, D, FF), D ** -0.5, 0.09375, ((0, 128), (1, 8)))
    w_up = centred(key_of[5], (EXPERTS, D, FF), D ** -0.5, 0.09375, ((0, 128), (1, 8)))
    w_down = centred(key_of[6], (EXPERTS, FF, D), (16 * FF) ** -0.5, 0.046875, ((0, 128), (2, 8)))
    return dict(tokens=tokens, grad_out=grad_out, gates=gates, expert_ids=expert_ids, w_gate=w_gate, w_up=w_up, w_down=w_down)


def node_slots(expert_ids):
    grouped = expert_ids.reshape(N_NODE, TOK_NODE * TOPK).astype(jnp.int32)
    onehot = (grouped[:, :, None] == jnp.arange(EXPERTS, dtype=jnp.int32)[None, None, :]).astype(jnp.int32)
    slot_rank = jnp.sum(onehot * (jnp.cumsum(onehot, axis=1) - 1), axis=2)
    return grouped, slot_rank.astype(jnp.int32)


def reference(tokens, grad_out, gates, expert_ids, w_gate, w_up, w_down):
    grouped, slot_rank = node_slots(expert_ids)
    source = jnp.broadcast_to(jnp.arange(N_NODE, dtype=jnp.int32)[:, None], grouped.shape)
    position = (source * CAP + slot_rank).reshape(-1).astype(jnp.int32)
    owner = grouped.reshape(-1).astype(jnp.int32)
    pair_index = jnp.arange(TOKENS * TOPK, dtype=jnp.int32)
    slot_table = jnp.zeros((EXPERTS, N_NODE * CAP), jnp.int32).at[owner, position].set(pair_index)
    slot_valid = jnp.zeros((EXPERTS, N_NODE * CAP), jnp.float32).at[owner, position].set(1.0)
    gate_flat = gates.reshape(-1)

    def expert_step(running, expert):
        grad_sum, gate_grads = running
        pairs = slot_table[expert]
        token_index = (pairs // TOPK).astype(jnp.int32)
        valid = slot_valid[expert]
        x_rows = jnp.take(tokens, token_index, axis=0)
        dy_rows = jnp.take(grad_out, token_index, axis=0)
        gate_pre = jnp.dot(x_rows, w_gate[expert], preferred_element_type=jnp.float32)
        up_pre = jnp.dot(x_rows, w_up[expert], preferred_element_type=jnp.float32)
        back_pre = lax.dot_general(dy_rows, w_down[expert], (((1,), (1,)), ((), ())), preferred_element_type=jnp.float32)
        sigmoid_gate = jax.nn.sigmoid(gate_pre)
        act = gate_pre * sigmoid_gate
        gate_part = jnp.sum(act * up_pre * back_pre, axis=1).astype(jnp.bfloat16)
        grad_up = (back_pre * act).astype(jnp.bfloat16)
        grad_gate = (back_pre * up_pre * sigmoid_gate * (1.0 + gate_pre * (1.0 - sigmoid_gate))).astype(jnp.bfloat16)
        row_grads = lax.dot_general(grad_gate, w_gate[expert], (((1,), (1,)), ((), ())), preferred_element_type=jnp.float32)
        row_grads = row_grads + lax.dot_general(grad_up, w_up[expert], (((1,), (1,)), ((), ())), preferred_element_type=jnp.float32)
        row_grads = row_grads.astype(jnp.bfloat16)
        weight = jnp.take(gate_flat, pairs) * valid
        grad_sum = grad_sum.at[token_index].add(weight[:, None] * row_grads.astype(jnp.float32))
        gate_grads = gate_grads.at[pairs].add(valid * gate_part.astype(jnp.float32))
        return (grad_sum, gate_grads), None

    start_state = (jnp.zeros((TOKENS, D), jnp.float32), jnp.zeros((TOKENS * TOPK,), jnp.float32))
    final, unused = lax.scan(expert_step, start_state, jnp.arange(EXPERTS, dtype=jnp.int32))
    grad_sum, gate_grads = final
    return grad_sum.astype(jnp.bfloat16), gate_grads.reshape(TOKENS, TOPK).astype(jnp.bfloat16)
```

```python
import functools

import jax
import jax.numpy as jnp
from jax import lax
from jax.experimental import pallas as pl
from jax.experimental.pallas import tpu as pltpu
from jax.sharding import PartitionSpec as P

BF16 = jnp.bfloat16
F32 = jnp.float32
VMEM = pl.BlockSpec(memory_space=pltpu.VMEM)
LIMIT = 40 * 1024 * 1024


def slot_choice(ids, slots, capacity):
    rows, top_count = ids.shape
    slot = lax.broadcasted_iota(jnp.int32, (rows, slots), 1)
    expert = slot // capacity
    named = jnp.zeros((rows, slots), F32)
    for k in range(top_count):
        named = named + jnp.where(ids[:, k : k + 1] == expert, 1.0, 0.0)
    before = lax.broadcasted_iota(jnp.int32, (rows, rows), 0) > lax.broadcasted_iota(
        jnp.int32, (rows, rows), 1
    )
    rank = jnp.dot(before.astype(BF16), named.astype(BF16), preferred_element_type=F32)
    return jnp.where(rank == (slot % capacity).astype(F32), named, 0.0), expert


def send_kernel(capacity, ids, tokens, grad_out, out):
    slots = out.shape[0]
    cols = tokens.shape[1]
    chosen, _ = slot_choice(ids[...], slots, capacity)
    chosen = chosen.astype(BF16)
    pick = (((0,), (0,)), ((), ()))
    out[:, :cols] = lax.dot_general(chosen, tokens[...], pick, preferred_element_type=F32).astype(BF16)
    out[:, cols:] = lax.dot_general(chosen, grad_out[...], pick, preferred_element_type=F32).astype(BF16)


def partial_kernel(n_local, index, rows_in, w_gate, w_up, w_down, *refs):
    outs, total = refs[:n_local], refs[n_local]
    cols = w_gate.shape[0]
    hidden = w_gate.shape[1]
    step = outs[0].shape[0]
    x = rows_in[:, :cols]
    dy = rows_in[:, cols:]
    total[:, :hidden] = jnp.dot(x, w_gate[...], preferred_element_type=F32)
    total[:, hidden : 2 * hidden] = jnp.dot(x, w_up[...], preferred_element_type=F32)
    total[:, 2 * hidden :] = lax.dot_general(
        dy, w_down[...], (((1,), (1,)), ((), ())), preferred_element_type=F32
    )
    me = index[0]
    for d in range(n_local):
        place = pl.multiple_of(lax.rem(me + d, n_local) * step, step)
        outs[d][...] = total[pl.ds(place, step), :].astype(outs[d].dtype)


def hidden_kernel(*refs):
    parts, out = refs[:-1], refs[-1]
    hidden = parts[0].shape[1] // 3

    def summed(start):
        value = parts[0][:, start : start + hidden].astype(F32)
        for part in parts[1:]:
            value = value + part[:, start : start + hidden].astype(F32)
        return value

    gate_pre, up_pre, back_pre = summed(0), summed(hidden), summed(2 * hidden)
    sigmoid_gate = jax.nn.sigmoid(gate_pre)
    act = gate_pre * sigmoid_gate
    grad_up = back_pre * act
    out[:, :hidden] = (
        back_pre * up_pre * sigmoid_gate * (1.0 + gate_pre * (1.0 - sigmoid_gate))
    ).astype(BF16)
    out[:, hidden : 2 * hidden] = grad_up.astype(BF16)
    gate_total = jnp.sum(grad_up * up_pre, axis=1, keepdims=True)
    extra = out.shape[1] - 2 * hidden
    out[:, 2 * hidden :] = jnp.broadcast_to(gate_total, (out.shape[0], extra)).astype(BF16)


def back_kernel(n_local, index, *refs):
    parts = refs[:n_local]
    w_gate, w_up, out, joined = refs[n_local:]
    cols, hidden = w_gate.shape
    step = parts[0].shape[0]
    me = index[0]
    for d in range(n_local):
        place = pl.multiple_of(lax.rem(me + n_local - d, n_local) * step, step)
        joined[pl.ds(place, step), :] = parts[d][...]
    across = (((1,), (1,)), ((), ()))
    result = lax.dot_general(joined[:, :hidden], w_gate[...], across, preferred_element_type=F32)
    result = result + lax.dot_general(
        joined[:, hidden : 2 * hidden], w_up[...], across, preferred_element_type=F32
    )
    out[:, :cols] = result.astype(BF16)
    out[:, cols:] = joined[:, 2 * hidden :]


def combine_kernel(capacity, ids, gates, rows_back, grad_tokens, grad_gates):
    slots = rows_back.shape[0]
    rows, cols = grad_tokens.shape
    top_count = gates.shape[1]
    named = ids[...]
    chosen, expert = slot_choice(named, slots, capacity)
    weight = jnp.zeros((rows, slots), F32)
    lane = lax.broadcasted_iota(jnp.int32, (rows, top_count), 1)
    values = jnp.zeros((rows, top_count), F32)
    for k in range(top_count):
        here = jnp.where(named[:, k : k + 1] == expert, chosen, 0.0)
        weight = weight + here * gates[:, k : k + 1]
        value = jnp.dot(here.astype(BF16), rows_back[:, cols:], preferred_element_type=F32)
        values = values + jnp.where(lane == k, value[:, :1], 0.0)
    high = weight.astype(BF16)
    rest = weight - high.astype(F32)
    middle = rest.astype(BF16)
    low = (rest - middle.astype(F32)).astype(BF16)
    total = jnp.zeros((rows, cols), F32)
    for part in (low, middle, high):
        total = total + jnp.dot(part, rows_back[:, :cols], preferred_element_type=F32)
    grad_tokens[...] = total.astype(BF16)
    grad_gates[...] = values.astype(BF16)


def on_device(tokens, grad_out, gates, expert_ids, w_gate, w_up, w_down):
    n_node = lax.axis_size("node")
    n_local = lax.axis_size("local")
    tok_rows, cols = tokens.shape
    top_count = expert_ids.shape[1]
    capacity = min(tok_rows, max(2, 2 * tok_rows * top_count // n_node))
    slots = n_node * capacity
    step = slots // n_local
    hidden = w_gate.shape[2]
    extra = 128
    shape = jax.ShapeDtypeStruct
    index = lax.axis_index("local").astype(jnp.int32).reshape(1)
    smem = pl.BlockSpec(memory_space=pltpu.SMEM)

    def build(kernel, out_shape, in_specs, flops, moved, scratch=()):
        return pl.pallas_call(
            kernel,
            out_shape=out_shape,
            in_specs=in_specs,
            out_specs=jax.tree.map(lambda _: VMEM, out_shape),
            scratch_shapes=list(scratch),
            compiler_params=pltpu.CompilerParams(vmem_limit_bytes=LIMIT),
            cost_estimate=pl.CostEstimate(flops=flops, bytes_accessed=moved, transcendentals=0),
        )

    outgoing = build(
        functools.partial(send_kernel, capacity),
        shape((slots, 2 * cols), BF16),
        [VMEM] * 3,
        2 * slots * tok_rows * 2 * cols,
        4 * slots * cols,
    )(expert_ids, tokens, grad_out)
    incoming = lax.all_to_all(
        outgoing.reshape(n_node, capacity, 2 * cols), "node", split_axis=0, concat_axis=0, tiled=True
    ).reshape(slots, 2 * cols)

    partials = build(
        functools.partial(partial_kernel, n_local),
        [shape((step, 3 * hidden), BF16) for _ in range(n_local)],
        [smem] + [VMEM] * 4,
        6 * slots * cols * hidden,
        2 * (3 * cols * hidden + slots * (2 * cols + 3 * hidden)),
        [pltpu.VMEM((slots, 3 * hidden), F32)],
    )(index, incoming, w_gate[0], w_up[0], w_down[0])

    def shifted(value, d):
        return lax.ppermute(value, "local", [(k, (k + d) % n_local) for k in range(n_local)])

    arrived = [partials[0]] + [shifted(partials[d], d) for d in range(1, n_local)]
    mine = build(
        hidden_kernel,
        shape((step, 2 * hidden + extra), BF16),
        [VMEM] * n_local,
        40 * step * hidden,
        2 * step * hidden * (3 * n_local + 2),
    )(*arrived)
    gathered = [mine] + [shifted(mine, d) for d in range(1, n_local)]
    sent = build(
        functools.partial(back_kernel, n_local),
        shape((slots, cols + extra), BF16),
        [smem] + [VMEM] * (n_local + 2),
        4 * slots * cols * hidden,
        2 * (2 * cols * hidden + slots * (2 * hidden + cols)),
        [pltpu.VMEM((slots, 2 * hidden + extra), BF16)],
    )(index, *gathered, w_gate[0], w_up[0])
    back = lax.all_to_all(
        sent.reshape(n_node, capacity, cols + extra), "node", split_axis=0, concat_axis=0, tiled=True
    ).reshape(slots, cols + extra)
    grad_tokens, grad_gates = build(
        functools.partial(combine_kernel, capacity),
        [shape((tok_rows, cols), BF16), shape((tok_rows, top_count), BF16)],
        [VMEM] * 3,
        8 * tok_rows * slots * cols,
        2 * slots * cols,
    )(expert_ids, gates, back)
    return grad_tokens, grad_gates


def solution(mesh):
    in_specs = (
        P("node", "local"),
        P("node", "local"),
        P("node", None),
        P("node", None),
        P("node", "local", None),
        P("node", "local", None),
        P("node", None, "local"),
    )
    out_specs = (P("node", "local"), P("node", None))
    return jax.shard_map(
        on_device, mesh=mesh, in_specs=in_specs, out_specs=out_specs, check_vma=False
    )
```

```python
import functools

import jax
import jax.numpy as jnp
from jax import lax
from jax.experimental import pallas as pl
from jax.experimental.pallas import tpu as pltpu
from jax.sharding import PartitionSpec as P

BF16 = jnp.bfloat16
F32 = jnp.float32
VMEM = pl.BlockSpec(memory_space=pltpu.VMEM)
LIMIT = 40 * 1024 * 1024


def slot_choice(ids, slots, capacity):
    top_count, rows = ids.shape
    slot = lax.broadcasted_iota(jnp.int32, (slots, rows), 0)
    expert = slot // capacity
    named = jnp.zeros((slots, rows), F32)
    for k in range(top_count):
        named = named + jnp.where(ids[k : k + 1, :] == expert, 1.0, 0.0)
    before = lax.broadcasted_iota(jnp.int32, (rows, rows), 0) < lax.broadcasted_iota(
        jnp.int32, (rows, rows), 1
    )
    before = jnp.where(before, 1.0, 0.0).astype(BF16)
    rank = jnp.dot(named.astype(BF16), before, preferred_element_type=F32)
    return jnp.where(rank == (slot % capacity).astype(F32), named, 0.0), expert


def send_kernel(capacity, ids, tokens, grad_out, out):
    slots = out.shape[0]
    cols = tokens.shape[1]
    chosen, _ = slot_choice(ids[...], slots, capacity)
    chosen = chosen.astype(BF16)
    out[:, :cols] = jnp.dot(chosen, tokens[...], preferred_element_type=F32).astype(BF16)
    out[:, cols:] = jnp.dot(chosen, grad_out[...], preferred_element_type=F32).astype(BF16)


def partial_kernel(order, index, rows_in, w_gate, w_up, w_down, *refs):
    n_local = len(order)
    outs = refs[:n_local]
    total = refs[n_local]
    cols = w_gate.shape[0]
    hidden = w_gate.shape[1]
    step = outs[0].shape[0]
    x = rows_in[:, :cols]
    dy = rows_in[:, cols:]
    total[:, :hidden] = jnp.dot(x, w_gate[...], preferred_element_type=F32)
    total[:, hidden : 2 * hidden] = jnp.dot(x, w_up[...], preferred_element_type=F32)
    total[:, 2 * hidden :] = lax.dot_general(
        dy, w_down[...], (((1,), (1,)), ((), ())), preferred_element_type=F32
    )
    me = index[0]
    for d, out in zip(order, outs):
        place = pl.multiple_of(lax.rem(me + d, n_local) * step, step)
        out[...] = total[pl.ds(place, step), :].astype(out.dtype)


def hidden_kernel(*refs):
    parts, out = refs[:-1], refs[-1]
    hidden = parts[0].shape[1] // 3

    def summed(start):
        value = parts[0][:, start : start + hidden].astype(F32)
        for part in parts[1:]:
            value = value + part[:, start : start + hidden].astype(F32)
        return value

    gate_pre, up_pre, back_pre = summed(0), summed(hidden), summed(2 * hidden)
    sigmoid_gate = jax.nn.sigmoid(gate_pre)
    act = gate_pre * sigmoid_gate
    grad_up = back_pre * act
    out[:, :hidden] = (
        back_pre * up_pre * sigmoid_gate * (1.0 + gate_pre * (1.0 - sigmoid_gate))
    ).astype(BF16)
    out[:, hidden : 2 * hidden] = grad_up.astype(BF16)
    gate_total = jnp.sum(grad_up * up_pre, axis=1, keepdims=True)
    extra = out.shape[1] - 2 * hidden
    out[:, 2 * hidden :] = jnp.broadcast_to(gate_total, (out.shape[0], extra)).astype(BF16)


def back_kernel(order, index, *refs):
    n_local = len(order)
    parts = refs[:n_local]
    w_gate, w_up, out, joined = refs[n_local:]
    cols, hidden = w_gate.shape
    step = parts[0].shape[0]
    me = index[0]
    for d, part in zip(order, parts):
        place = pl.multiple_of(lax.rem(me + n_local - d, n_local) * step, step)
        joined[pl.ds(place, step), :] = part[...]
    across = (((1,), (1,)), ((), ()))
    result = lax.dot_general(joined[:, :hidden], w_gate[...], across, preferred_element_type=F32)
    result = result + lax.dot_general(
        joined[:, hidden : 2 * hidden], w_up[...], across, preferred_element_type=F32
    )
    out[:, :cols] = result.astype(BF16)
    out[:, cols:] = joined[:, 2 * hidden :]


def combine_kernel(capacity, ids, gates, rows_back, grad_tokens, grad_gates):
    slots = rows_back.shape[0]
    rows, cols = grad_tokens.shape
    top_count = gates.shape[0]
    named = ids[...]
    chosen, expert = slot_choice(named, slots, capacity)
    weight = jnp.zeros((slots, rows), F32)
    across = (((0,), (0,)), ((), ()))
    for k in range(top_count):
        here = jnp.where(named[k : k + 1, :] == expert, chosen, 0.0)
        weight = weight + here * gates[k : k + 1, :]
        value = lax.dot_general(
            rows_back[:, cols:], here.astype(BF16), across, preferred_element_type=F32
        )
        grad_gates[k : k + 1, :] = value[:1, :].astype(BF16)
    high = weight.astype(BF16)
    rest = weight - high.astype(F32)
    middle = rest.astype(BF16)
    low = (rest - middle.astype(F32)).astype(BF16)
    total = jnp.zeros((rows, cols), F32)
    for part in (low, middle, high):
        total = total + lax.dot_general(
            part, rows_back[:, :cols], across, preferred_element_type=F32
        )
    grad_tokens[...] = total.astype(BF16)


def ring_order(n):
    order = [0] + ([n // 2] if n % 2 == 0 and n > 1 else [])
    for d in range((n - 1) // 2, 0, -1):
        order += [d, n - d]
    return order


def on_device(tokens, grad_out, gates, expert_ids, w_gate, w_up, w_down):
    n_node = lax.axis_size("node")
    n_local = lax.axis_size("local")
    tok_rows, cols = tokens.shape
    top_count = expert_ids.shape[1]
    capacity = min(tok_rows, max(2, 2 * tok_rows * top_count // n_node))
    slots = n_node * capacity
    step = slots // n_local
    hidden = w_gate.shape[2]
    extra = 128
    shape = jax.ShapeDtypeStruct
    index = lax.axis_index("local").astype(jnp.int32).reshape(1)
    smem = pl.BlockSpec(memory_space=pltpu.SMEM)
    order = ring_order(n_local)
    named = expert_ids.T

    def build(kernel, out_shape, in_specs, flops, moved, scratch=()):
        return pl.pallas_call(
            kernel,
            out_shape=out_shape,
            in_specs=in_specs,
            out_specs=jax.tree.map(lambda _: VMEM, out_shape),
            scratch_shapes=list(scratch),
            compiler_params=pltpu.CompilerParams(vmem_limit_bytes=LIMIT),
            cost_estimate=pl.CostEstimate(flops=flops, bytes_accessed=moved, transcendentals=0),
        )

    outgoing = build(
        functools.partial(send_kernel, capacity),
        shape((slots, 2 * cols), BF16),
        [VMEM] * 3,
        2 * slots * tok_rows * 2 * cols,
        4 * slots * cols,
    )(named, tokens, grad_out)
    incoming = lax.all_to_all(
        outgoing.reshape(n_node, capacity, 2 * cols), "node", split_axis=0, concat_axis=0, tiled=True
    ).reshape(slots, 2 * cols)

    partials = build(
        functools.partial(partial_kernel, order),
        [shape((step, 3 * hidden), BF16) for _ in range(n_local)],
        [smem] + [VMEM] * 4,
        6 * slots * cols * hidden,
        2 * (3 * cols * hidden + slots * (2 * cols + 3 * hidden)),
        [pltpu.VMEM((slots, 3 * hidden), F32)],
    )(index, incoming, w_gate[0], w_up[0], w_down[0])

    def shifted(value, d):
        return lax.ppermute(value, "local", [(k, (k + d) % n_local) for k in range(n_local)])

    arrived = [shifted(part, d) if d else part for d, part in zip(order, partials)]
    mine = build(
        hidden_kernel,
        shape((step, 2 * hidden + extra), BF16),
        [VMEM] * n_local,
        40 * step * hidden,
        2 * step * hidden * (3 * n_local + 2),
    )(*arrived)
    gathered = [shifted(mine, d) if d else mine for d in reversed(order)]
    sent = build(
        functools.partial(back_kernel, order[::-1]),
        shape((slots, cols + extra), BF16),
        [smem] + [VMEM] * (n_local + 2),
        4 * slots * cols * hidden,
        2 * (2 * cols * hidden + slots * (2 * hidden + cols)),
        [pltpu.VMEM((slots, 2 * hidden + extra), BF16)],
    )(index, *gathered, w_gate[0], w_up[0])
    back = lax.all_to_all(
        sent.reshape(n_node, capacity, cols + extra), "node", split_axis=0, concat_axis=0, tiled=True
    ).reshape(slots, cols + extra)
    grad_tokens, grad_gates = build(
        functools.partial(combine_kernel, capacity),
        [shape((tok_rows, cols), BF16), shape((top_count, tok_rows), BF16)],
        [VMEM] * 3,
        8 * tok_rows * slots * cols,
        2 * slots * cols,
    )(named, gates.T, back)
    return grad_tokens, grad_gates.T


def solution(mesh):
    in_specs = (
        P("node", "local"),
        P("node", "local"),
        P("node", None),
        P("node", None),
        P("node", "local", None),
        P("node", "local", None),
        P("node", None, "local"),
    )
    out_specs = (P("node", "local"), P("node", None))
    return jax.shard_map(
        on_device, mesh=mesh, in_specs=in_specs, out_specs=out_specs, check_vma=False
    )
```

```python
import functools

import jax
import jax.numpy as jnp
from jax import lax
from jax.experimental import pallas as pl
from jax.experimental.pallas import tpu as pltpu
from jax.sharding import PartitionSpec as P

BF16 = jnp.bfloat16
F32 = jnp.float32
VMEM = pl.BlockSpec(memory_space=pltpu.VMEM)
LIMIT = 40 * 1024 * 1024
RIGHT, LEFT, FAR, KEPT = (2, 4), 6, 5, (1, 3, 7)


def slot_choice(ids, slots, capacity):
    top_count, rows = ids.shape
    slot = lax.broadcasted_iota(jnp.int32, (slots, rows), 0)
    expert = slot // capacity
    named = jnp.zeros((slots, rows), F32)
    for k in range(top_count):
        named = named + jnp.where(ids[k : k + 1, :] == expert, 1.0, 0.0)
    before = lax.broadcasted_iota(jnp.int32, (rows, rows), 0) < lax.broadcasted_iota(
        jnp.int32, (rows, rows), 1
    )
    before = jnp.where(before, 1.0, 0.0).astype(BF16)
    rank = jnp.dot(named.astype(BF16), before, preferred_element_type=F32)
    return jnp.where(rank == (slot % capacity).astype(F32), named, 0.0), expert


def send_kernel(capacity, ids, tokens, grad_out, out, ids_here, tokens_here, grads_here, sems):
    slots = out.shape[0] * capacity
    cols = tokens.shape[1]
    copies = [
        pltpu.make_async_copy(source, target, sems.at[i])
        for i, (source, target) in enumerate(
            [(ids, ids_here), (tokens, tokens_here), (grad_out, grads_here)]
        )
    ]
    for copy in copies:
        copy.start()
    copies[0].wait()
    chosen, _ = slot_choice(ids_here[...], slots, capacity)
    chosen = chosen.astype(BF16)
    copies[1].wait()
    picked = jnp.dot(chosen, tokens_here[...], preferred_element_type=F32).astype(BF16)
    out[:, :, :cols] = picked.reshape(out.shape[0], capacity, cols)
    copies[2].wait()
    picked = jnp.dot(chosen, grads_here[...], preferred_element_type=F32).astype(BF16)
    out[:, :, cols:] = picked.reshape(out.shape[0], capacity, cols)


def partial_kernel(n_local, index, rows_in, w_gate, w_up, w_down, *refs):
    mine, kept, right, left, far, total = refs
    cols, hidden = w_gate.shape
    step = mine.shape[0]
    x = rows_in[:, :cols]
    dy = rows_in[:, cols:]
    total[:, :hidden] = jnp.dot(x, w_gate[...], preferred_element_type=F32)
    total[:, hidden : 2 * hidden] = jnp.dot(x, w_up[...], preferred_element_type=F32)
    total[:, 2 * hidden :] = lax.dot_general(
        dy, w_down[...], (((1,), (1,)), ((), ())), preferred_element_type=F32
    )
    me = index[0]

    def chunk(d):
        place = pl.multiple_of(lax.rem(me + d, n_local) * step, step)
        return total[pl.ds(place, step), :]

    mine[...] = chunk(0)
    for i, d in enumerate(KEPT):
        kept[i * step : (i + 1) * step, :] = chunk(d)
    for i, d in enumerate(RIGHT):
        right[i * step : (i + 1) * step, :] = chunk(d).astype(BF16)
    left[...] = chunk(LEFT).astype(BF16)
    far[...] = chunk(FAR).astype(BF16)


def hidden_kernel(*refs):
    parts, out = refs[:-1], refs[-1]
    hidden = parts[0].shape[1] // 3

    def summed(start):
        value = parts[0][:, start : start + hidden].astype(F32)
        for part in parts[1:]:
            value = value + part[:, start : start + hidden].astype(F32)
        return value

    gate_pre, up_pre, back_pre = summed(0), summed(hidden), summed(2 * hidden)
    sigmoid_gate = jax.nn.sigmoid(gate_pre)
    act = gate_pre * sigmoid_gate
    grad_up = back_pre * act
    out[:, :hidden] = (
        back_pre * up_pre * sigmoid_gate * (1.0 + gate_pre * (1.0 - sigmoid_gate))
    ).astype(BF16)
    out[:, hidden : 2 * hidden] = grad_up.astype(BF16)
    gate_total = jnp.sum(grad_up * up_pre, axis=1, keepdims=True)
    extra = out.shape[1] - 2 * hidden
    out[:, 2 * hidden :] = jnp.broadcast_to(gate_total, (out.shape[0], extra)).astype(BF16)


def back_kernel(order, index, *refs):
    n_local = len(order)
    parts = refs[:n_local]
    w_gate, w_up, out, joined = refs[n_local:]
    cols, hidden = w_gate.shape
    step = parts[0].shape[0]
    me = index[0]
    for d, part in zip(order, parts):
        place = pl.multiple_of(lax.rem(me + n_local - d, n_local) * step, step)
        joined[pl.ds(place, step), :] = part[...]
    across = (((1,), (1,)), ((), ()))
    result = lax.dot_general(joined[:, :hidden], w_gate[...], across, preferred_element_type=F32)
    result = result + lax.dot_general(
        joined[:, hidden : 2 * hidden], w_up[...], across, preferred_element_type=F32
    )
    out[:, :cols] = result.astype(BF16)
    out[:, cols:] = joined[:, 2 * hidden :]


def combine_kernel(capacity, ids, gates, rows_back, grad_tokens, grad_gates):
    slots = rows_back.shape[0]
    rows, cols = grad_tokens.shape
    top_count = gates.shape[0]
    named = ids[...]
    chosen, expert = slot_choice(named, slots, capacity)
    weight = jnp.zeros((slots, rows), F32)
    across = (((0,), (0,)), ((), ()))
    for k in range(top_count):
        here = jnp.where(named[k : k + 1, :] == expert, chosen, 0.0)
        weight = weight + here * gates[k : k + 1, :]
        value = lax.dot_general(
            rows_back[:, cols:], here.astype(BF16), across, preferred_element_type=F32
        )
        grad_gates[k : k + 1, :] = value[:1, :].astype(BF16)
    high = weight.astype(BF16)
    rest = weight - high.astype(F32)
    middle = rest.astype(BF16)
    low = (rest - middle.astype(F32)).astype(BF16)
    total = jnp.zeros((rows, cols), F32)
    for part in (low, middle, high):
        total = total + lax.dot_general(
            part, rows_back[:, :cols], across, preferred_element_type=F32
        )
    grad_tokens[...] = total.astype(BF16)


def ring_order(n):
    order = [0] + ([n // 2] if n % 2 == 0 and n > 1 else [])
    for d in range((n - 1) // 2, 0, -1):
        order += [d, n - d]
    return order


def on_device(tokens, grad_out, gates, expert_ids, w_gate, w_up, w_down):
    n_node = lax.axis_size("node")
    n_local = lax.axis_size("local")
    tok_rows, cols = tokens.shape
    top_count = expert_ids.shape[1]
    capacity = min(tok_rows, max(2, 2 * tok_rows * top_count // n_node))
    slots = n_node * capacity
    step = slots // n_local
    hidden = w_gate.shape[2]
    extra = 128
    shape = jax.ShapeDtypeStruct
    index = lax.axis_index("local").astype(jnp.int32).reshape(1)
    smem = pl.BlockSpec(memory_space=pltpu.SMEM)
    anywhere = pl.BlockSpec(memory_space=pl.ANY)
    order = ring_order(n_local)
    named = expert_ids.T

    def build(kernel, out_shape, in_specs, flops, moved, scratch=(), limit=LIMIT):
        return pl.pallas_call(
            kernel,
            out_shape=out_shape,
            in_specs=in_specs,
            out_specs=jax.tree.map(lambda _: VMEM, out_shape),
            scratch_shapes=list(scratch),
            compiler_params=pltpu.CompilerParams(vmem_limit_bytes=limit),
            cost_estimate=pl.CostEstimate(flops=flops, bytes_accessed=moved, transcendentals=0),
        )

    outgoing = build(
        functools.partial(send_kernel, capacity),
        shape((n_node, capacity, 2 * cols), BF16),
        [anywhere] * 3,
        2 * slots * tok_rows * 2 * cols,
        4 * slots * cols,
        [
            pltpu.VMEM((top_count, tok_rows), jnp.int32),
            pltpu.VMEM((tok_rows, cols), BF16),
            pltpu.VMEM((tok_rows, cols), BF16),
            pltpu.SemaphoreType.DMA((3,)),
        ],
        limit=63 * 1024 * 1024,
    )(named, tokens, grad_out)
    incoming = lax.all_to_all(
        outgoing, "node", split_axis=0, concat_axis=0, tiled=True
    ).reshape(slots, 2 * cols)

    mine, kept, right, left, far = build(
        functools.partial(partial_kernel, n_local),
        [
            shape((step, 3 * hidden), F32),
            shape((len(KEPT) * step, 3 * hidden), F32),
            shape((len(RIGHT) * step, 3 * hidden), BF16),
            shape((step, 3 * hidden), BF16),
            shape((step, 3 * hidden), BF16),
        ],
        [smem] + [VMEM] * 4,
        6 * slots * cols * hidden,
        2 * (3 * cols * hidden + slots * (2 * cols + 3 * hidden)),
        [pltpu.VMEM((slots, 3 * hidden), F32)],
    )(index, incoming, w_gate[0], w_up[0], w_down[0])

    def shifted(value, d):
        return lax.ppermute(value, "local", [(k, (k + d) % n_local) for k in range(n_local)])

    def added(sent, place):
        return (sent.astype(F32) + kept[place * step : (place + 1) * step]).astype(BF16)

    from_right = shifted(left, n_local - 1)
    from_left = shifted(right, 1)
    arrived = [
        shifted(far, FAR),
        shifted(added(from_right, 2), KEPT[2]),
        shifted(added(from_left[:step], 0), KEPT[0]),
        shifted(added(from_left[step:], 1), KEPT[1]),
    ]
    hidden_grads = build(
        hidden_kernel,
        shape((step, 2 * hidden + extra), BF16),
        [VMEM] * 5,
        40 * step * hidden,
        2 * step * hidden * (3 * n_local + 2),
    )(mine, *arrived)
    gathered = [shifted(hidden_grads, d) if d else hidden_grads for d in reversed(order)]
    sent = build(
        functools.partial(back_kernel, order[::-1]),
        shape((slots, cols + extra), BF16),
        [smem] + [VMEM] * (n_local + 2),
        4 * slots * cols * hidden,
        2 * (2 * cols * hidden + slots * (2 * hidden + cols)),
        [pltpu.VMEM((slots, 2 * hidden + extra), BF16)],
    )(index, *gathered, w_gate[0], w_up[0])
    back = lax.all_to_all(
        sent.reshape(n_node, capacity, cols + extra), "node", split_axis=0, concat_axis=0, tiled=True
    ).reshape(slots, cols + extra)
    grad_tokens, grad_gates = build(
        functools.partial(combine_kernel, capacity),
        [shape((tok_rows, cols), BF16), shape((top_count, tok_rows), BF16)],
        [VMEM] * 3,
        8 * tok_rows * slots * cols,
        2 * slots * cols,
    )(named, gates.T, back)
    return grad_tokens, grad_gates.T


def solution(mesh):
    in_specs = (
        P("node", "local"),
        P("node", "local"),
        P("node", None),
        P("node", None),
        P("node", "local", None),
        P("node", "local", None),
        P("node", None, "local"),
    )
    out_specs = (P("node", "local"), P("node", None))
    return jax.shard_map(
        on_device, mesh=mesh, in_specs=in_specs, out_specs=out_specs, check_vma=False
    )
```

```python
import functools

import jax
import jax.numpy as jnp
from jax import lax
from jax.experimental import pallas as pl
from jax.experimental.pallas import tpu as pltpu
from jax.sharding import PartitionSpec as P

BF16 = jnp.bfloat16
F32 = jnp.float32
VMEM = pl.BlockSpec(memory_space=pltpu.VMEM)
LIMIT = 40 * 1024 * 1024
RING = 8
BY_RIGHT, BY_LEFT, KEPT = (4, 6, 1), (2, 7), (3, 5)
FROM_HERE, FROM_LEFT, FROM_RIGHT = (0, 5, 3), (7, 4, 2), (1, 6)


def slot_choice(ids, slots, capacity):
    top_count, rows = ids.shape
    slot = lax.broadcasted_iota(jnp.int32, (slots, rows), 0)
    expert = slot // capacity
    named = jnp.zeros((slots, rows), F32)
    for k in range(top_count):
        named = named + jnp.where(ids[k : k + 1, :] == expert, 1.0, 0.0)
    before = lax.broadcasted_iota(jnp.int32, (rows, rows), 0) < lax.broadcasted_iota(
        jnp.int32, (rows, rows), 1
    )
    before = jnp.where(before, 1.0, 0.0).astype(BF16)
    rank = jnp.dot(named.astype(BF16), before, preferred_element_type=F32)
    return jnp.where(rank == (slot % capacity).astype(F32), named, 0.0), expert


def send_kernel(capacity, ids, tokens, grad_out, out, ids_here, tokens_here, grads_here, sems):
    slots = out.shape[0] * capacity
    cols = tokens.shape[1]
    copies = [
        pltpu.make_async_copy(source, target, sems.at[i])
        for i, (source, target) in enumerate(
            [(ids, ids_here), (tokens, tokens_here), (grad_out, grads_here)]
        )
    ]
    for copy in copies:
        copy.start()
    copies[0].wait()
    chosen, _ = slot_choice(ids_here[...], slots, capacity)
    chosen = chosen.astype(BF16)
    copies[1].wait()
    picked = jnp.dot(chosen, tokens_here[...], preferred_element_type=F32).astype(BF16)
    out[:, :, :cols] = picked.reshape(out.shape[0], capacity, cols)
    copies[2].wait()
    picked = jnp.dot(chosen, grads_here[...], preferred_element_type=F32).astype(BF16)
    out[:, :, cols:] = picked.reshape(out.shape[0], capacity, cols)


def partial_kernel(n_local, index, rows_in, w_gate, w_up, w_down, *refs):
    mine, kept, right, left, total = refs
    cols, hidden = w_gate.shape
    step = mine.shape[0]
    x = rows_in[:, :cols]
    dy = rows_in[:, cols:]
    total[:, :hidden] = jnp.dot(x, w_gate[...], preferred_element_type=F32)
    total[:, hidden : 2 * hidden] = jnp.dot(x, w_up[...], preferred_element_type=F32)
    total[:, 2 * hidden :] = lax.dot_general(
        dy, w_down[...], (((1,), (1,)), ((), ())), preferred_element_type=F32
    )
    me = index[0]

    def chunk(d):
        place = pl.multiple_of(lax.rem(me + d, n_local) * step, step)
        return total[pl.ds(place, step), :]

    mine[...] = chunk(0)
    for out, distances in ((kept, KEPT), (right, BY_RIGHT), (left, BY_LEFT)):
        for i, d in enumerate(distances):
            out[i * step : (i + 1) * step, :] = chunk(d).astype(out.dtype)


def hidden_kernel(mine, from_left, from_right, by_three, by_five, out):
    hidden = mine.shape[1] // 3
    step = out.shape[0]

    def summed(start):
        at = pl.ds(start, hidden)
        value = mine[:, at] + from_left[2 * step : 3 * step, at].astype(F32)
        value = value + from_right[step : 2 * step, at].astype(F32)
        return value + by_three[:, at].astype(F32) + by_five[:, at].astype(F32)

    gate_pre, up_pre, back_pre = summed(0), summed(hidden), summed(2 * hidden)
    sigmoid_gate = jax.nn.sigmoid(gate_pre)
    act = gate_pre * sigmoid_gate
    grad_up = back_pre * act
    out[:, :hidden] = (
        back_pre * up_pre * sigmoid_gate * (1.0 + gate_pre * (1.0 - sigmoid_gate))
    ).astype(BF16)
    out[:, hidden : 2 * hidden] = grad_up.astype(BF16)
    gate_total = jnp.sum(grad_up * up_pre, axis=1, keepdims=True)
    extra = out.shape[1] - 2 * hidden
    out[:, 2 * hidden :] = jnp.broadcast_to(gate_total, (out.shape[0], extra)).astype(BF16)


def back_kernel(n_local, index, here, by_three, by_five, from_left, from_right, w_gate, w_up, out, joined):
    cols, hidden = w_gate.shape
    step = here.shape[0]
    me = index[0]

    def place(d, part, i):
        at = pl.multiple_of(lax.rem(me + d, n_local) * step, step)
        joined[pl.ds(at, step), :] = part[i * step : (i + 1) * step, :]

    for d, part in zip(FROM_HERE, (here, by_three, by_five)):
        place(d, part, 0)
    for i, d in enumerate(FROM_LEFT):
        place(d, from_left, i)
    for i, d in enumerate(FROM_RIGHT):
        place(d, from_right, i)
    across = (((1,), (1,)), ((), ()))
    result = lax.dot_general(joined[:, :hidden], w_gate[...], across, preferred_element_type=F32)
    result = result + lax.dot_general(
        joined[:, hidden : 2 * hidden], w_up[...], across, preferred_element_type=F32
    )
    out[:, :cols] = result.astype(BF16)
    out[:, cols:] = joined[:, 2 * hidden :]


def combine_kernel(capacity, ids, gates, rows_back, grad_tokens, grad_gates):
    slots = rows_back.shape[0]
    rows, cols = grad_tokens.shape
    top_count = gates.shape[0]
    named = ids[...]
    chosen, expert = slot_choice(named, slots, capacity)
    weight = jnp.zeros((slots, rows), F32)
    across = (((0,), (0,)), ((), ()))
    for k in range(top_count):
        here = jnp.where(named[k : k + 1, :] == expert, chosen, 0.0)
        weight = weight + here * gates[k : k + 1, :]
        value = lax.dot_general(
            rows_back[:, cols:], here.astype(BF16), across, preferred_element_type=F32
        )
        grad_gates[k : k + 1, :] = value[:1, :].astype(BF16)
    high = weight.astype(BF16)
    rest = weight - high.astype(F32)
    middle = rest.astype(BF16)
    low = (rest - middle.astype(F32)).astype(BF16)
    total = jnp.zeros((rows, cols), F32)
    for part in (low, middle, high):
        total = total + lax.dot_general(
            part, rows_back[:, :cols], across, preferred_element_type=F32
        )
    grad_tokens[...] = total.astype(BF16)


def on_device(tokens, grad_out, gates, expert_ids, w_gate, w_up, w_down):
    n_node = lax.axis_size("node")
    n_local = lax.axis_size("local")
    tok_rows, cols = tokens.shape
    top_count = expert_ids.shape[1]
    capacity = min(tok_rows, max(2, 2 * tok_rows * top_count // n_node))
    slots = n_node * capacity
    step = slots // n_local
    hidden = w_gate.shape[2]
    extra = 128
    shape = jax.ShapeDtypeStruct
    index = lax.axis_index("local").astype(jnp.int32).reshape(1)
    smem = pl.BlockSpec(memory_space=pltpu.SMEM)
    anywhere = pl.BlockSpec(memory_space=pl.ANY)
    assert n_local == RING
    named = expert_ids.T

    def build(kernel, out_shape, in_specs, flops, moved, scratch=(), limit=LIMIT):
        return pl.pallas_call(
            kernel,
            out_shape=out_shape,
            in_specs=in_specs,
            out_specs=jax.tree.map(lambda _: VMEM, out_shape),
            scratch_shapes=list(scratch),
            compiler_params=pltpu.CompilerParams(vmem_limit_bytes=limit),
            cost_estimate=pl.CostEstimate(flops=flops, bytes_accessed=moved, transcendentals=0),
        )

    outgoing = build(
        functools.partial(send_kernel, capacity),
        shape((n_node, capacity, 2 * cols), BF16),
        [anywhere] * 3,
        2 * slots * tok_rows * 2 * cols,
        4 * slots * cols,
        [
            pltpu.VMEM((top_count, tok_rows), jnp.int32),
            pltpu.VMEM((tok_rows, cols), BF16),
            pltpu.VMEM((tok_rows, cols), BF16),
            pltpu.SemaphoreType.DMA((3,)),
        ],
        limit=63 * 1024 * 1024,
    )(named, tokens, grad_out)
    incoming = lax.all_to_all(
        outgoing, "node", split_axis=0, concat_axis=0, tiled=True
    ).reshape(slots, 2 * cols)

    mine, kept, right, left = build(
        functools.partial(partial_kernel, n_local),
        [
            shape((step, 3 * hidden), F32),
            shape((len(KEPT) * step, 3 * hidden), F32),
            shape((len(BY_RIGHT) * step, 3 * hidden), BF16),
            shape((len(BY_LEFT) * step, 3 * hidden), BF16),
        ],
        [smem] + [VMEM] * 4,
        6 * slots * cols * hidden,
        2 * (3 * cols * hidden + slots * (2 * cols + 3 * hidden)),
        [pltpu.VMEM((slots, 3 * hidden), F32)],
    )(index, incoming, w_gate[0], w_up[0], w_down[0])

    def shifted(value, d):
        return lax.ppermute(value, "local", [(k, (k + d) % n_local) for k in range(n_local)])

    from_left = shifted(right, 1)
    from_right = shifted(left, n_local - 1)
    by_five = shifted((kept[step:] + from_left[step : 2 * step].astype(F32)).astype(BF16), 5)
    by_three = kept[:step] + from_left[:step].astype(F32) + from_right[:step].astype(F32)
    by_three = shifted(by_three.astype(BF16), 3)
    hidden_grads = build(
        hidden_kernel,
        shape((step, 2 * hidden + extra), BF16),
        [VMEM] * 5,
        40 * step * hidden,
        2 * step * hidden * (3 * n_local + 2),
    )(mine, from_left, from_right, by_three, by_five)
    by_five = shifted(hidden_grads, 5)
    by_three = shifted(hidden_grads, 3)
    from_right = shifted(jnp.concatenate([hidden_grads, by_three], axis=0), n_local - 1)
    from_left = shifted(jnp.concatenate([hidden_grads, by_three, by_five], axis=0), 1)
    sent = build(
        functools.partial(back_kernel, n_local),
        shape((slots, cols + extra), BF16),
        [smem] + [VMEM] * 7,
        4 * slots * cols * hidden,
        2 * (2 * cols * hidden + slots * (2 * hidden + cols)),
        [pltpu.VMEM((slots, 2 * hidden + extra), BF16)],
    )(index, hidden_grads, by_three, by_five, from_left, from_right, w_gate[0], w_up[0])
    back = lax.all_to_all(
        sent.reshape(n_node, capacity, cols + extra), "node", split_axis=0, concat_axis=0, tiled=True
    ).reshape(slots, cols + extra)
    grad_tokens, grad_gates = build(
        functools.partial(combine_kernel, capacity),
        [shape((tok_rows, cols), BF16), shape((top_count, tok_rows), BF16)],
        [VMEM] * 3,
        8 * tok_rows * slots * cols,
        2 * slots * cols,
    )(named, gates.T, back)
    return grad_tokens, grad_gates.T


def solution(mesh):
    in_specs = (
        P("node", "local"),
        P("node", "local"),
        P("node", None),
        P("node", None),
        P("node", "local", None),
        P("node", "local", None),
        P("node", None, "local"),
    )
    out_specs = (P("node", "local"), P("node", None))
    return jax.shard_map(
        on_device, mesh=mesh, in_specs=in_specs, out_specs=out_specs, check_vma=False
    )
```

```python
import functools

import jax
import jax.numpy as jnp
from jax import lax
from jax.experimental import pallas as pl
from jax.experimental.pallas import tpu as pltpu
from jax.sharding import PartitionSpec as P

BF16 = jnp.bfloat16
F32 = jnp.float32
VMEM = pl.BlockSpec(memory_space=pltpu.VMEM)
LIMIT = 40 * 1024 * 1024
RIGHT, LEFT, FAR, KEPT = (2, 4), 6, 5, (1, 3, 7)


def slot_choice(ids, slots, capacity):
    top_count, rows = ids.shape
    slot = lax.broadcasted_iota(jnp.int32, (slots, rows), 0)
    expert = slot // capacity
    named = jnp.zeros((slots, rows), F32)
    for k in range(top_count):
        named = named + jnp.where(ids[k : k + 1, :] == expert, 1.0, 0.0)
    before = lax.broadcasted_iota(jnp.int32, (rows, rows), 0) < lax.broadcasted_iota(
        jnp.int32, (rows, rows), 1
    )
    before = jnp.where(before, 1.0, 0.0).astype(BF16)
    rank = jnp.dot(named.astype(BF16), before, preferred_element_type=F32)
    return jnp.where(rank == (slot % capacity).astype(F32), named, 0.0), expert


def send_kernel(capacity, ids, tokens, grad_out, out, ids_here, tokens_here, grads_here, sems):
    slots = out.shape[0] * capacity
    cols = tokens.shape[1]
    copies = [
        pltpu.make_async_copy(source, target, sems.at[i])
        for i, (source, target) in enumerate(
            [(ids, ids_here), (tokens, tokens_here), (grad_out, grads_here)]
        )
    ]
    for copy in copies:
        copy.start()
    copies[0].wait()
    chosen, _ = slot_choice(ids_here[...], slots, capacity)
    chosen = chosen.astype(BF16)
    copies[1].wait()
    picked = jnp.dot(chosen, tokens_here[...], preferred_element_type=F32).astype(BF16)
    out[:, :, :cols] = picked.reshape(out.shape[0], capacity, cols)
    copies[2].wait()
    picked = jnp.dot(chosen, grads_here[...], preferred_element_type=F32).astype(BF16)
    out[:, :, cols:] = picked.reshape(out.shape[0], capacity, cols)


def partial_kernel(n_local, index, rows_in, w_gate, w_up, w_down, *refs):
    mine, kept, right, left, far, total = refs
    cols, hidden = w_gate.shape
    step = mine.shape[0]
    x = rows_in[:, :cols]
    dy = rows_in[:, cols:]
    total[:, :hidden] = jnp.dot(x, w_gate[...], preferred_element_type=F32)
    total[:, hidden : 2 * hidden] = jnp.dot(x, w_up[...], preferred_element_type=F32)
    total[:, 2 * hidden :] = lax.dot_general(
        dy, w_down[...], (((1,), (1,)), ((), ())), preferred_element_type=F32
    )
    me = index[0]

    def chunk(d):
        place = pl.multiple_of(lax.rem(me + d, n_local) * step, step)
        return total[pl.ds(place, step), :]

    mine[...] = chunk(0)
    for i, d in enumerate(KEPT):
        kept[i * step : (i + 1) * step, :] = chunk(d)
    for i, d in enumerate(RIGHT):
        right[i * step : (i + 1) * step, :] = chunk(d).astype(BF16)
    left[...] = chunk(LEFT).astype(BF16)
    far[...] = chunk(FAR).astype(BF16)


def hidden_kernel(*refs):
    parts, out = refs[:-1], refs[-1]
    hidden = parts[0].shape[1] // 3

    def summed(start):
        value = parts[0][:, start : start + hidden].astype(F32)
        for part in parts[1:]:
            value = value + part[:, start : start + hidden].astype(F32)
        return value

    gate_pre, up_pre, back_pre = summed(0), summed(hidden), summed(2 * hidden)
    sigmoid_gate = jax.nn.sigmoid(gate_pre)
    act = gate_pre * sigmoid_gate
    grad_up = back_pre * act
    grad_gate = (
        back_pre * up_pre * sigmoid_gate * (1.0 + gate_pre * (1.0 - sigmoid_gate))
    ).astype(BF16)
    grad_up_sent = grad_up.astype(BF16)
    gate_total = jnp.sum(grad_up * up_pre, axis=1, keepdims=True)
    copies, step, width = out.shape
    gate_total = jnp.broadcast_to(gate_total, (step, width - 2 * hidden)).astype(BF16)
    for i in range(copies):
        out[i, :, :hidden] = grad_gate
        out[i, :, hidden : 2 * hidden] = grad_up_sent
        out[i, :, 2 * hidden :] = gate_total


def back_kernel(joined, w_gate, w_up, out):
    cols, hidden = w_gate.shape
    across = (((1,), (1,)), ((), ()))
    result = lax.dot_general(joined[:, :hidden], w_gate[...], across, preferred_element_type=F32)
    result = result + lax.dot_general(
        joined[:, hidden : 2 * hidden], w_up[...], across, preferred_element_type=F32
    )
    out[:, :cols] = result.astype(BF16)
    out[:, cols:] = joined[:, 2 * hidden :]


def weight_kernel(capacity, ids, gates, weights, places):
    slots = weights.shape[0]
    top_count, rows = gates.shape
    named = ids[...]
    chosen, expert = slot_choice(named, slots, capacity)
    weight = jnp.zeros((slots, rows), F32)
    for k in range(top_count):
        here = jnp.where(named[k : k + 1, :] == expert, chosen, 0.0)
        weight = weight + here * gates[k : k + 1, :]
        places[:, k * rows : (k + 1) * rows] = here.astype(BF16)
    high = weight.astype(BF16)
    rest = weight - high.astype(F32)
    middle = rest.astype(BF16)
    low = (rest - middle.astype(F32)).astype(BF16)
    for i, part in enumerate((low, middle, high)):
        weights[:, i * rows : (i + 1) * rows] = part


def combine_kernel(weights, places, rows_back, grad_tokens, grad_gates):
    rows, cols = grad_tokens.shape
    across = (((0,), (0,)), ((), ()))
    values = lax.dot_general(rows_back[:, cols:], places[...], across, preferred_element_type=F32)
    for k in range(grad_gates.shape[0]):
        grad_gates[k : k + 1, :] = values[:1, k * rows : (k + 1) * rows].astype(BF16)
    parts = lax.dot_general(weights[...], rows_back[:, :cols], across, preferred_element_type=F32)
    total = parts[:rows] + parts[rows : 2 * rows] + parts[2 * rows :]
    grad_tokens[...] = total.astype(BF16)


def on_device(tokens, grad_out, gates, expert_ids, w_gate, w_up, w_down):
    n_node = lax.axis_size("node")
    n_local = lax.axis_size("local")
    tok_rows, cols = tokens.shape
    top_count = expert_ids.shape[1]
    capacity = min(tok_rows, max(2, 2 * tok_rows * top_count // n_node))
    slots = n_node * capacity
    step = slots // n_local
    hidden = w_gate.shape[2]
    extra = 128
    shape = jax.ShapeDtypeStruct
    index = lax.axis_index("local").astype(jnp.int32).reshape(1)
    smem = pl.BlockSpec(memory_space=pltpu.SMEM)
    anywhere = pl.BlockSpec(memory_space=pl.ANY)
    assert n_local == 8
    named = expert_ids.T

    def build(kernel, out_shape, in_specs, flops, moved, scratch=(), limit=LIMIT):
        return pl.pallas_call(
            kernel,
            out_shape=out_shape,
            in_specs=in_specs,
            out_specs=jax.tree.map(lambda _: VMEM, out_shape),
            scratch_shapes=list(scratch),
            compiler_params=pltpu.CompilerParams(vmem_limit_bytes=limit),
            cost_estimate=pl.CostEstimate(flops=flops, bytes_accessed=moved, transcendentals=0),
        )

    outgoing = build(
        functools.partial(send_kernel, capacity),
        shape((n_node, capacity, 2 * cols), BF16),
        [anywhere] * 3,
        2 * slots * tok_rows * 2 * cols,
        4 * slots * cols,
        [
            pltpu.VMEM((top_count, tok_rows), jnp.int32),
            pltpu.VMEM((tok_rows, cols), BF16),
            pltpu.VMEM((tok_rows, cols), BF16),
            pltpu.SemaphoreType.DMA((3,)),
        ],
        limit=63 * 1024 * 1024,
    )(named, tokens, grad_out)
    weights, places = build(
        functools.partial(weight_kernel, capacity),
        [shape((slots, 3 * tok_rows), BF16), shape((slots, top_count * tok_rows), BF16)],
        [VMEM] * 2,
        100 * slots * tok_rows * top_count,
        2 * slots * tok_rows * (top_count + 3),
    )(named, gates.T)
    incoming = lax.all_to_all(
        outgoing, "node", split_axis=0, concat_axis=0, tiled=True
    ).reshape(slots, 2 * cols)

    mine, kept, right, left, far = build(
        functools.partial(partial_kernel, n_local),
        [
            shape((step, 3 * hidden), F32),
            shape((len(KEPT) * step, 3 * hidden), F32),
            shape((len(RIGHT) * step, 3 * hidden), BF16),
            shape((step, 3 * hidden), BF16),
            shape((step, 3 * hidden), BF16),
        ],
        [smem] + [VMEM] * 4,
        6 * slots * cols * hidden,
        2 * (3 * cols * hidden + slots * (2 * cols + 3 * hidden)),
        [pltpu.VMEM((slots, 3 * hidden), F32)],
    )(index, incoming, w_gate[0], w_up[0], w_down[0])

    def shifted(value, d):
        return lax.ppermute(value, "local", [(k, (k + d) % n_local) for k in range(n_local)])

    def added(sent, place):
        return (sent.astype(F32) + kept[place * step : (place + 1) * step]).astype(BF16)

    from_right = shifted(left, n_local - 1)
    from_left = shifted(right, 1)
    arrived = [
        shifted(far, FAR),
        shifted(added(from_left[step:], 1), KEPT[1]),
        shifted(added(from_left[:step], 0), KEPT[0]),
        shifted(added(from_right, 2), KEPT[2]),
    ]
    copies = build(
        hidden_kernel,
        shape((n_local, step, 2 * hidden + extra), BF16),
        [VMEM] * 5,
        40 * step * hidden,
        2 * step * hidden * (3 * n_local + 2 * n_local),
    )(mine, *arrived)
    gathered = lax.all_to_all(copies, "local", split_axis=0, concat_axis=0, tiled=True)
    sent = build(
        back_kernel,
        shape((slots, cols + extra), BF16),
        [VMEM] * 3,
        4 * slots * cols * hidden,
        2 * (2 * cols * hidden + slots * (2 * hidden + cols)),
    )(gathered.reshape(slots, 2 * hidden + extra), w_gate[0], w_up[0])
    back = lax.all_to_all(
        sent.reshape(n_node, capacity, cols + extra), "node", split_axis=0, concat_axis=0, tiled=True
    ).reshape(slots, cols + extra)
    grad_tokens, grad_gates = build(
        combine_kernel,
        [shape((tok_rows, cols), BF16), shape((top_count, tok_rows), BF16)],
        [VMEM] * 3,
        8 * tok_rows * slots * cols,
        2 * slots * cols,
    )(weights, places, back)
    return grad_tokens, grad_gates.T


def solution(mesh):
    in_specs = (
        P("node", "local"),
        P("node", "local"),
        P("node", None),
        P("node", None),
        P("node", "local", None),
        P("node", "local", None),
        P("node", None, "local"),
    )
    out_specs = (P("node", "local"), P("node", None))
    return jax.shard_map(
        on_device, mesh=mesh, in_specs=in_specs, out_specs=out_specs, check_vma=False
    )
```

```python
import functools

import jax
import jax.numpy as jnp
from jax import lax
from jax.experimental import pallas as pl
from jax.experimental.pallas import tpu as pltpu
from jax.sharding import PartitionSpec as P

BF16 = jnp.bfloat16
F32 = jnp.float32
VMEM = pl.BlockSpec(memory_space=pltpu.VMEM)
LIMIT = 40 * 1024 * 1024
RIGHT, LEFT, FAR, KEPT = (2, 4), 6, 5, (1, 3, 7)
FROM_HERE, FROM_LEFT, FROM_RIGHT = (0, 5, 3), (7, 4, 2), (1, 6)


def slot_choice(ids, slots, capacity):
    top_count, rows = ids.shape
    slot = lax.broadcasted_iota(jnp.int32, (slots, rows), 0)
    expert = slot // capacity
    named = jnp.zeros((slots, rows), F32)
    for k in range(top_count):
        named = named + jnp.where(ids[k : k + 1, :] == expert, 1.0, 0.0)
    before = lax.broadcasted_iota(jnp.int32, (rows, rows), 0) < lax.broadcasted_iota(
        jnp.int32, (rows, rows), 1
    )
    before = jnp.where(before, 1.0, 0.0).astype(BF16)
    rank = jnp.dot(named.astype(BF16), before, preferred_element_type=F32)
    return jnp.where(rank == (slot % capacity).astype(F32), named, 0.0), expert


def send_kernel(capacity, ids, tokens, grad_out, out, ids_here, tokens_here, grads_here, sems):
    slots = out.shape[0] * capacity
    cols = tokens.shape[1]
    copies = [
        pltpu.make_async_copy(source, target, sems.at[i])
        for i, (source, target) in enumerate(
            [(ids, ids_here), (tokens, tokens_here), (grad_out, grads_here)]
        )
    ]
    for copy in copies:
        copy.start()
    copies[0].wait()
    chosen, _ = slot_choice(ids_here[...], slots, capacity)
    chosen = chosen.astype(BF16)
    copies[1].wait()
    picked = jnp.dot(chosen, tokens_here[...], preferred_element_type=F32).astype(BF16)
    out[:, :, :cols] = picked.reshape(out.shape[0], capacity, cols)
    copies[2].wait()
    picked = jnp.dot(chosen, grads_here[...], preferred_element_type=F32).astype(BF16)
    out[:, :, cols:] = picked.reshape(out.shape[0], capacity, cols)


def partial_kernel(n_local, index, rows_in, w_gate, w_up, w_down, first, *refs):
    del first
    mine, kept, right, left, far, total = refs
    cols, hidden = w_gate.shape
    step = mine.shape[0]
    x = rows_in[:, :cols]
    dy = rows_in[:, cols:]
    total[:, :hidden] = jnp.dot(x, w_gate[...], preferred_element_type=F32)
    total[:, hidden : 2 * hidden] = jnp.dot(x, w_up[...], preferred_element_type=F32)
    total[:, 2 * hidden :] = lax.dot_general(
        dy, w_down[...], (((1,), (1,)), ((), ())), preferred_element_type=F32
    )
    me = index[0]

    def chunk(d):
        place = pl.multiple_of(lax.rem(me + d, n_local) * step, step)
        return total[pl.ds(place, step), :]

    mine[...] = chunk(0)
    for i, d in enumerate(KEPT):
        kept[i * step : (i + 1) * step, :] = chunk(d)
    for i, d in enumerate(RIGHT):
        right[i * step : (i + 1) * step, :] = chunk(d).astype(BF16)
    left[...] = chunk(LEFT).astype(BF16)
    far[...] = chunk(FAR).astype(BF16)


def hidden_kernel(*refs):
    parts, out = refs[:-1], refs[-1]
    hidden = parts[0].shape[1] // 3

    def summed(start):
        value = parts[0][:, start : start + hidden].astype(F32)
        for part in parts[1:]:
            value = value + part[:, start : start + hidden].astype(F32)
        return value

    gate_pre, up_pre, back_pre = summed(0), summed(hidden), summed(2 * hidden)
    sigmoid_gate = jax.nn.sigmoid(gate_pre)
    act = gate_pre * sigmoid_gate
    grad_up = back_pre * act
    out[:, :hidden] = (
        back_pre * up_pre * sigmoid_gate * (1.0 + gate_pre * (1.0 - sigmoid_gate))
    ).astype(BF16)
    out[:, hidden : 2 * hidden] = grad_up.astype(BF16)
    gate_total = jnp.sum(grad_up * up_pre, axis=1, keepdims=True)
    extra = out.shape[1] - 2 * hidden
    out[:, 2 * hidden :] = jnp.broadcast_to(gate_total, (out.shape[0], extra)).astype(BF16)


def back_kernel(n_local, index, here, by_three, by_five, from_left, from_right, w_gate, w_up, out, joined):
    cols, hidden = w_gate.shape
    step = here.shape[0]
    me = index[0]

    def place(d, part, i):
        at = pl.multiple_of(lax.rem(me + d, n_local) * step, step)
        joined[pl.ds(at, step), :] = part[i * step : (i + 1) * step, :]

    for d, part in zip(FROM_HERE, (here, by_three, by_five)):
        place(d, part, 0)
    for i, d in enumerate(FROM_LEFT):
        place(d, from_left, i)
    for i, d in enumerate(FROM_RIGHT):
        place(d, from_right, i)
    across = (((1,), (1,)), ((), ()))
    result = lax.dot_general(joined[:, :hidden], w_gate[...], across, preferred_element_type=F32)
    result = result + lax.dot_general(
        joined[:, hidden : 2 * hidden], w_up[...], across, preferred_element_type=F32
    )
    out[:, :cols] = result.astype(BF16)
    out[:, cols:] = joined[:, 2 * hidden :]


def weight_kernel(capacity, ids, gates, weights, places):
    slots = weights.shape[0]
    top_count, rows = gates.shape
    named = ids[...]
    chosen, expert = slot_choice(named, slots, capacity)
    weight = jnp.zeros((slots, rows), F32)
    for k in range(top_count):
        here = jnp.where(named[k : k + 1, :] == expert, chosen, 0.0)
        weight = weight + here * gates[k : k + 1, :]
        places[:, k * rows : (k + 1) * rows] = here.astype(BF16)
    high = weight.astype(BF16)
    rest = weight - high.astype(F32)
    middle = rest.astype(BF16)
    low = (rest - middle.astype(F32)).astype(BF16)
    for i, part in enumerate((low, middle, high)):
        weights[:, i * rows : (i + 1) * rows] = part


def combine_kernel(weights, places, rows_back, grad_tokens, grad_gates):
    rows, cols = grad_tokens.shape
    across = (((0,), (0,)), ((), ()))
    values = lax.dot_general(rows_back[:, cols:], places[...], across, preferred_element_type=F32)
    for k in range(grad_gates.shape[0]):
        grad_gates[k : k + 1, :] = values[:1, k * rows : (k + 1) * rows].astype(BF16)
    parts = lax.dot_general(weights[...], rows_back[:, :cols], across, preferred_element_type=F32)
    total = parts[:rows] + parts[rows : 2 * rows] + parts[2 * rows :]
    grad_tokens[...] = total.astype(BF16)


def on_device(tokens, grad_out, gates, expert_ids, w_gate, w_up, w_down):
    n_node = lax.axis_size("node")
    n_local = lax.axis_size("local")
    tok_rows, cols = tokens.shape
    top_count = expert_ids.shape[1]
    capacity = min(tok_rows, max(2, 2 * tok_rows * top_count // n_node))
    slots = n_node * capacity
    step = slots // n_local
    hidden = w_gate.shape[2]
    extra = 128
    shape = jax.ShapeDtypeStruct
    index = lax.axis_index("local").astype(jnp.int32).reshape(1)
    smem = pl.BlockSpec(memory_space=pltpu.SMEM)
    anywhere = pl.BlockSpec(memory_space=pl.ANY)
    assert n_local == 8
    named = expert_ids.T

    def build(kernel, out_shape, in_specs, flops, moved, scratch=(), limit=LIMIT):
        return pl.pallas_call(
            kernel,
            out_shape=out_shape,
            in_specs=in_specs,
            out_specs=jax.tree.map(lambda _: VMEM, out_shape),
            scratch_shapes=list(scratch),
            compiler_params=pltpu.CompilerParams(vmem_limit_bytes=limit),
            cost_estimate=pl.CostEstimate(flops=flops, bytes_accessed=moved, transcendentals=0),
        )

    outgoing = build(
        functools.partial(send_kernel, capacity),
        shape((n_node, capacity, 2 * cols), BF16),
        [anywhere] * 3,
        2 * slots * tok_rows * 2 * cols,
        4 * slots * cols,
        [
            pltpu.VMEM((top_count, tok_rows), jnp.int32),
            pltpu.VMEM((tok_rows, cols), BF16),
            pltpu.VMEM((tok_rows, cols), BF16),
            pltpu.SemaphoreType.DMA((3,)),
        ],
        limit=63 * 1024 * 1024,
    )(named, tokens, grad_out)
    weights, places = build(
        functools.partial(weight_kernel, capacity),
        [shape((slots, 3 * tok_rows), BF16), shape((slots, top_count * tok_rows), BF16)],
        [VMEM] * 2,
        100 * slots * tok_rows * top_count,
        2 * slots * tok_rows * (top_count + 3),
    )(named, gates.T)
    incoming = lax.all_to_all(
        outgoing, "node", split_axis=0, concat_axis=0, tiled=True
    ).reshape(slots, 2 * cols)

    mine, kept, right, left, far = build(
        functools.partial(partial_kernel, n_local),
        [
            shape((step, 3 * hidden), F32),
            shape((len(KEPT) * step, 3 * hidden), F32),
            shape((len(RIGHT) * step, 3 * hidden), BF16),
            shape((step, 3 * hidden), BF16),
            shape((step, 3 * hidden), BF16),
        ],
        [smem] + [VMEM] * 4 + [anywhere],
        6 * slots * cols * hidden,
        2 * (3 * cols * hidden + slots * (2 * cols + 3 * hidden)),
        [pltpu.VMEM((slots, 3 * hidden), F32)],
    )(index, incoming, w_gate[0], w_up[0], w_down[0], weights)

    def shifted(value, d):
        return lax.ppermute(value, "local", [(k, (k + d) % n_local) for k in range(n_local)])

    def added(sent, place):
        return (sent.astype(F32) + kept[place * step : (place + 1) * step]).astype(BF16)

    from_right = shifted(left, n_local - 1)
    from_left = shifted(right, 1)
    arrived = [
        shifted(far, FAR),
        shifted(added(from_left[:step], 0), KEPT[0]),
        shifted(added(from_left[step:], 1), KEPT[1]),
        shifted(added(from_right, 2), KEPT[2]),
    ]
    hidden_grads = build(
        hidden_kernel,
        shape((step, 2 * hidden + extra), BF16),
        [VMEM] * 5,
        40 * step * hidden,
        2 * step * hidden * (3 * n_local + 2),
    )(mine, *arrived)
    by_five = shifted(hidden_grads, 5)
    by_three = shifted(hidden_grads, 3)
    from_right = shifted(jnp.concatenate([hidden_grads, by_three], axis=0), n_local - 1)
    from_left = shifted(jnp.concatenate([hidden_grads, by_three, by_five], axis=0), 1)
    sent = build(
        functools.partial(back_kernel, n_local),
        shape((slots, cols + extra), BF16),
        [smem] + [VMEM] * 7,
        4 * slots * cols * hidden,
        2 * (2 * cols * hidden + slots * (2 * hidden + cols)),
        [pltpu.VMEM((slots, 2 * hidden + extra), BF16)],
    )(index, hidden_grads, by_three, by_five, from_left, from_right, w_gate[0], w_up[0])
    back = lax.all_to_all(
        sent.reshape(n_node, capacity, cols + extra), "node", split_axis=0, concat_axis=0, tiled=True
    ).reshape(slots, cols + extra)
    grad_tokens, grad_gates = build(
        combine_kernel,
        [shape((tok_rows, cols), BF16), shape((top_count, tok_rows), BF16)],
        [VMEM] * 3,
        8 * tok_rows * slots * cols,
        2 * slots * cols,
    )(weights, places, back)
    return grad_tokens, grad_gates.T


def solution(mesh):
    in_specs = (
        P("node", "local"),
        P("node", "local"),
        P("node", None),
        P("node", None),
        P("node", "local", None),
        P("node", "local", None),
        P("node", None, "local"),
    )
    out_specs = (P("node", "local"), P("node", None))
    return jax.shard_map(
        on_device, mesh=mesh, in_specs=in_specs, out_specs=out_specs, check_vma=False
    )
```

```python
import functools

import jax
import jax.numpy as jnp
from jax import lax
from jax.experimental import pallas as pl
from jax.experimental.pallas import tpu as pltpu
from jax.sharding import PartitionSpec as P

BF16 = jnp.bfloat16
F32 = jnp.float32
VMEM = pl.BlockSpec(memory_space=pltpu.VMEM)
LIMIT = 40 * 1024 * 1024
RIGHT, LEFT, FAR, KEPT_RIGHT, KEPT_LEFT = (2, 4), 6, 5, (1, 3), 7
FROM_HERE, FROM_LEFT, FROM_RIGHT, FROM_RIGHT_LATE = (0, 5, 3), (7, 2), (1, 4), 6


def slot_choice(ids, slots, capacity):
    top_count, rows = ids.shape
    slot = lax.broadcasted_iota(jnp.int32, (slots, rows), 0)
    expert = slot // capacity
    named = jnp.zeros((slots, rows), F32)
    for k in range(top_count):
        named = named + jnp.where(ids[k : k + 1, :] == expert, 1.0, 0.0)
    before = lax.broadcasted_iota(jnp.int32, (rows, rows), 0) < lax.broadcasted_iota(
        jnp.int32, (rows, rows), 1
    )
    before = jnp.where(before, 1.0, 0.0).astype(BF16)
    rank = jnp.dot(named.astype(BF16), before, preferred_element_type=F32)
    return jnp.where(rank == (slot % capacity).astype(F32), named, 0.0), expert


def send_kernel(capacity, ids, tokens, grad_out, out, ids_here, tokens_here, grads_here, sems):
    slots = out.shape[0] * capacity
    cols = tokens.shape[1]
    copies = [
        pltpu.make_async_copy(source, target, sems.at[i])
        for i, (source, target) in enumerate(
            [(ids, ids_here), (tokens, tokens_here), (grad_out, grads_here)]
        )
    ]
    for copy in copies:
        copy.start()
    copies[0].wait()
    chosen, _ = slot_choice(ids_here[...], slots, capacity)
    chosen = chosen.astype(BF16)
    copies[1].wait()
    picked = jnp.dot(chosen, tokens_here[...], preferred_element_type=F32).astype(BF16)
    out[:, :, :cols] = picked.reshape(out.shape[0], capacity, cols)
    copies[2].wait()
    picked = jnp.dot(chosen, grads_here[...], preferred_element_type=F32).astype(BF16)
    out[:, :, cols:] = picked.reshape(out.shape[0], capacity, cols)


def partial_kernel(n_local, index, rows_in, w_gate, w_up, w_down, first, *refs):
    del first
    mine, kept_right, kept_left, right, left, far, total = refs
    cols, hidden = w_gate.shape
    step = mine.shape[0]
    x = rows_in[:, :cols]
    dy = rows_in[:, cols:]
    total[:, :hidden] = jnp.dot(x, w_gate[...], preferred_element_type=F32)
    total[:, hidden : 2 * hidden] = jnp.dot(x, w_up[...], preferred_element_type=F32)
    total[:, 2 * hidden :] = lax.dot_general(
        dy, w_down[...], (((1,), (1,)), ((), ())), preferred_element_type=F32
    )
    me = index[0]

    def chunk(d):
        place = pl.multiple_of(lax.rem(me + d, n_local) * step, step)
        return total[pl.ds(place, step), :]

    mine[...] = chunk(0)
    for i, d in enumerate(KEPT_RIGHT):
        kept_right[i * step : (i + 1) * step, :] = chunk(d)
    kept_left[...] = chunk(KEPT_LEFT)
    for i, d in enumerate(RIGHT):
        right[i * step : (i + 1) * step, :] = chunk(d).astype(BF16)
    left[...] = chunk(LEFT).astype(BF16)
    far[...] = chunk(FAR).astype(BF16)


def hidden_kernel(*refs):
    parts, out = refs[:-1], refs[-1]
    hidden = parts[0].shape[1] // 3

    def summed(start):
        value = parts[0][:, start : start + hidden].astype(F32)
        for part in parts[1:]:
            value = value + part[:, start : start + hidden].astype(F32)
        return value

    gate_pre, up_pre, back_pre = summed(0), summed(hidden), summed(2 * hidden)
    sigmoid_gate = jax.nn.sigmoid(gate_pre)
    act = gate_pre * sigmoid_gate
    grad_up = back_pre * act
    out[:, :hidden] = (
        back_pre * up_pre * sigmoid_gate * (1.0 + gate_pre * (1.0 - sigmoid_gate))
    ).astype(BF16)
    out[:, hidden : 2 * hidden] = grad_up.astype(BF16)
    gate_total = jnp.sum(grad_up * up_pre, axis=1, keepdims=True)
    extra = out.shape[1] - 2 * hidden
    out[:, 2 * hidden :] = jnp.broadcast_to(gate_total, (out.shape[0], extra)).astype(BF16)


def back_kernel(n_local, index, here, by_three, by_five, from_left, from_right, late, w_gate, w_up, out, joined):
    cols, hidden = w_gate.shape
    step = here.shape[0]
    me = index[0]

    def place(d, part, i):
        at = pl.multiple_of(lax.rem(me + d, n_local) * step, step)
        joined[pl.ds(at, step), :] = part[i * step : (i + 1) * step, :]

    for d, part in zip(FROM_HERE, (here, by_three, by_five)):
        place(d, part, 0)
    for i, d in enumerate(FROM_LEFT):
        place(d, from_left, i)
    for i, d in enumerate(FROM_RIGHT):
        place(d, from_right, i)
    place(FROM_RIGHT_LATE, late, 0)
    across = (((1,), (1,)), ((), ()))
    result = lax.dot_general(joined[:, :hidden], w_gate[...], across, preferred_element_type=F32)
    result = result + lax.dot_general(
        joined[:, hidden : 2 * hidden], w_up[...], across, preferred_element_type=F32
    )
    out[:, :cols] = result.astype(BF16)
    out[:, cols:] = joined[:, 2 * hidden :]


def weight_kernel(capacity, ids, gates, weights, places):
    slots = weights.shape[0]
    top_count, rows = gates.shape
    named = ids[...]
    chosen, expert = slot_choice(named, slots, capacity)
    weight = jnp.zeros((slots, rows), F32)
    for k in range(top_count):
        here = jnp.where(named[k : k + 1, :] == expert, chosen, 0.0)
        weight = weight + here * gates[k : k + 1, :]
        places[:, k * rows : (k + 1) * rows] = here.astype(BF16)
    high = weight.astype(BF16)
    rest = weight - high.astype(F32)
    middle = rest.astype(BF16)
    low = (rest - middle.astype(F32)).astype(BF16)
    for i, part in enumerate((low, middle, high)):
        weights[:, i * rows : (i + 1) * rows] = part


def combine_kernel(weights, places, rows_back, grad_tokens, grad_gates):
    rows, cols = grad_tokens.shape
    across = (((0,), (0,)), ((), ()))
    values = lax.dot_general(rows_back[:, cols:], places[...], across, preferred_element_type=F32)
    for k in range(grad_gates.shape[0]):
        grad_gates[k : k + 1, :] = values[:1, k * rows : (k + 1) * rows].astype(BF16)
    parts = lax.dot_general(weights[...], rows_back[:, :cols], across, preferred_element_type=F32)
    total = parts[:rows] + parts[rows : 2 * rows] + parts[2 * rows :]
    grad_tokens[...] = total.astype(BF16)


def on_device(tokens, grad_out, gates, expert_ids, w_gate, w_up, w_down):
    n_node = lax.axis_size("node")
    n_local = lax.axis_size("local")
    tok_rows, cols = tokens.shape
    top_count = expert_ids.shape[1]
    capacity = min(tok_rows, max(2, 2 * tok_rows * top_count // n_node))
    slots = n_node * capacity
    step = slots // n_local
    hidden = w_gate.shape[2]
    extra = 128
    shape = jax.ShapeDtypeStruct
    index = lax.axis_index("local").astype(jnp.int32).reshape(1)
    smem = pl.BlockSpec(memory_space=pltpu.SMEM)
    anywhere = pl.BlockSpec(memory_space=pl.ANY)
    assert n_local == 8
    named = expert_ids.T

    def build(kernel, out_shape, in_specs, flops, moved, scratch=(), limit=LIMIT):
        return pl.pallas_call(
            kernel,
            out_shape=out_shape,
            in_specs=in_specs,
            out_specs=jax.tree.map(lambda _: VMEM, out_shape),
            scratch_shapes=list(scratch),
            compiler_params=pltpu.CompilerParams(vmem_limit_bytes=limit),
            cost_estimate=pl.CostEstimate(flops=flops, bytes_accessed=moved, transcendentals=0),
        )

    outgoing = build(
        functools.partial(send_kernel, capacity),
        shape((n_node, capacity, 2 * cols), BF16),
        [anywhere] * 3,
        2 * slots * tok_rows * 2 * cols,
        4 * slots * cols,
        [
            pltpu.VMEM((top_count, tok_rows), jnp.int32),
            pltpu.VMEM((tok_rows, cols), BF16),
            pltpu.VMEM((tok_rows, cols), BF16),
            pltpu.SemaphoreType.DMA((3,)),
        ],
        limit=63 * 1024 * 1024,
    )(named, tokens, grad_out)
    weights, places = build(
        functools.partial(weight_kernel, capacity),
        [shape((slots, 3 * tok_rows), BF16), shape((slots, top_count * tok_rows), BF16)],
        [VMEM] * 2,
        100 * slots * tok_rows * top_count,
        2 * slots * tok_rows * (top_count + 3),
    )(named, gates.T)
    incoming = lax.all_to_all(
        outgoing, "node", split_axis=0, concat_axis=0, tiled=True
    ).reshape(slots, 2 * cols)

    mine, kept_right, kept_left, right, left, far = build(
        functools.partial(partial_kernel, n_local),
        [
            shape((step, 3 * hidden), F32),
            shape((len(KEPT_RIGHT) * step, 3 * hidden), F32),
            shape((step, 3 * hidden), F32),
            shape((len(RIGHT) * step, 3 * hidden), BF16),
            shape((step, 3 * hidden), BF16),
            shape((step, 3 * hidden), BF16),
        ],
        [smem] + [VMEM] * 4 + [anywhere],
        6 * slots * cols * hidden,
        2 * (3 * cols * hidden + slots * (2 * cols + 3 * hidden)),
        [pltpu.VMEM((slots, 3 * hidden), F32)],
    )(index, incoming, w_gate[0], w_up[0], w_down[0], weights)

    def shifted(value, d):
        return lax.ppermute(value, "local", [(k, (k + d) % n_local) for k in range(n_local)])

    def added(sent, kept):
        return (sent.astype(F32) + kept).astype(BF16)

    from_left = shifted(right, 1)
    from_right = shifted(left, n_local - 1)
    arrived = [
        shifted(far, FAR),
        shifted(added(from_left[:step], kept_right[:step]), KEPT_RIGHT[0]),
        shifted(added(from_left[step:], kept_right[step:]), KEPT_RIGHT[1]),
        shifted(added(from_right, kept_left), KEPT_LEFT),
    ]
    hidden_grads = build(
        hidden_kernel,
        shape((step, 2 * hidden + extra), BF16),
        [VMEM] * 5,
        40 * step * hidden,
        2 * step * hidden * (3 * n_local + 2),
    )(mine, *arrived)
    by_five = shifted(hidden_grads, 5)
    by_three = shifted(hidden_grads, 3)
    both = jnp.concatenate([hidden_grads, by_five], axis=0)
    gathered_left = shifted(both, 1)
    gathered_right = shifted(both, n_local - 1)
    late = shifted(by_three, n_local - 1)
    sent = build(
        functools.partial(back_kernel, n_local),
        shape((slots, cols + extra), BF16),
        [smem] + [VMEM] * 8,
        4 * slots * cols * hidden,
        2 * (2 * cols * hidden + slots * (2 * hidden + cols)),
        [pltpu.VMEM((slots, 2 * hidden + extra), BF16)],
    )(index, hidden_grads, by_three, by_five, gathered_left, gathered_right, late, w_gate[0], w_up[0])
    back = lax.all_to_all(
        sent.reshape(n_node, capacity, cols + extra), "node", split_axis=0, concat_axis=0, tiled=True
    ).reshape(slots, cols + extra)
    grad_tokens, grad_gates = build(
        combine_kernel,
        [shape((tok_rows, cols), BF16), shape((top_count, tok_rows), BF16)],
        [VMEM] * 3,
        8 * tok_rows * slots * cols,
        2 * slots * cols,
    )(weights, places, back)
    return grad_tokens, grad_gates.T


def solution(mesh):
    in_specs = (
        P("node", "local"),
        P("node", "local"),
        P("node", None),
        P("node", None),
        P("node", "local", None),
        P("node", "local", None),
        P("node", None, "local"),
    )
    out_specs = (P("node", "local"), P("node", None))
    return jax.shard_map(
        on_device, mesh=mesh, in_specs=in_specs, out_specs=out_specs, check_vma=False
    )
```
